1024 devices in a mesh: dp: 16 (over y, core), expert: 64 (over x, z).
Axes of the slice: x: 8, y: 8, z: 8, core: 2. Of those that a mesh axis runs over, the one named last changes fastest.
Arguments:
- grad_out: bfloat16 [131072, 2048], P(('dp', 'expert')), may hold values from -6 to 6
- route_ids: int32 [131072, 2], P(('dp', 'expert')), may hold values from 0 to 127, all different within a row; in each aligned block of 128 rows (0 to 127, 128 to 255, ...) at most 4 rows name the same one
- route_probs: float32 [131072, 2], P(('dp', 'expert')), may hold values from 0.01 to 0.3
- hidden: bfloat16 [16, 64, 128, 4, 768], P('dp', None, 'expert'), may hold values from -2 to 2
- w_down: bfloat16 [128, 768, 2048], P('expert'), may hold values from -0.21875 to 0.21875
Outputs:
- hidden_grad: bfloat16 [16, 64, 128, 4, 768], P('dp', None, 'expert')
- prob_grad: float32 [131072, 2], P(('dp', 'expert'))
- weight_grad: float32 [768, 128, 2048], P('dp', 'expert')
The draws below stay inside these ranges and needn't reach their ends.
Inputs may be any that keep to these rules, and one draw needn't show every extreme that they name: `route_ids`: each row names 2 different experts; among the 128 rows of one device no expert is named more than 4 times, a bound that some block reaches.
All inputs are finite; a program needn't handle non-finite values.
Results may differ from the reference program's by a relative error of at most 0.022.
Values may be sent and summed in bfloat16 or wider, within the bound.
A program may use at most 128 MiB of HBM per device.

```python
import math
import jax
import jax.numpy as jnp
import numpy as np
from jax import lax

D = 2048
H = 768
TOP = 2
TOK_DEV = 128
EXPERTS = 128
CAP = 4
TOKENS = 131072
N_DP = 16
N_EXPERT = 64


def strengthened(drawn, stream_key, source, target, blocks, factor):
    def block_of(dim):
        return (jnp.arange(drawn.shape[dim]) // (drawn.shape[dim] // blocks)).reshape((-1,) + (1,) * (drawn.ndim - 1 - dim))

    near = jax.random.permutation(stream_key, blocks)[block_of(target)]
    far = (block_of(target) + blocks // 2) % blocks
    return jnp.where((block_of(source) == near) | (block_of(source) == far), factor * drawn, drawn)


def steps_of(rng, shape, split, low, high):
    def one(dim, blocks):
        heights = jax.random.uniform(jax.random.fold_in(jax.random.fold_in(rng, 6), dim), (blocks,), jnp.float32, low / len(split), high / len(split))
        return jnp.repeat(jnp.exp(heights), shape[dim] // blocks).reshape((-1,) + (1,) * (len(shape) - dim - 1))

    factor_of = one(*split[0])
    for cut in split[1:]:
        factor_of = factor_of * one(*cut)
    return factor_of


def shared_out(key, own, number, rows, number_of, top, reach, skew):
    ranking = jax.random.permutation(key, number_of)
    packed, common = shares(number_of, rows * top, reach, skew, True), shares(number_of, rows * top, reach, skew, False)
    places = jnp.arange(number_of)

    def named(sizes, turn):
        used = int((sizes > 0).sum())
        fixed = max(1, used // 4)
        shifted = fixed + (places - fixed + turn * (used - fixed)) % max(1, number_of - fixed)
        return jnp.zeros((number_of,), jnp.int32).at[ranking[jnp.where(places < fixed, places, shifted)]].set(jnp.asarray(sizes, jnp.int32))

    sizes = jnp.where(number % 4 == 0, named(packed, number // 4), named(common, number - number // 4 - 1))
    mixed = jax.random.permutation(jax.random.fold_in(own, 3), number_of)
    source_of, sink = mixed[0:number_of // 2 * 2:2], mixed[1:number_of // 2 * 2:2]
    margin = jnp.minimum(sizes[source_of] - 1, reach - sizes[sink]) // 2
    margin = jnp.where((source_of == ranking[0]) | (sink == ranking[0]) | (sizes[sink] == 0), 0, jnp.maximum(margin, 0))
    shifted = jax.random.randint(jax.random.fold_in(own, 4), (number_of // 2,), 0, 1 << 20) % (margin + 1)
    sizes = sizes.at[source_of].add(-shifted).at[sink].add(shifted)
    labels = jnp.searchsorted(jnp.cumsum(sizes), jnp.arange(rows * top), side="right").astype(jnp.int32)
    grid = labels.reshape(top, rows).T
    grid = grid[jax.random.permutation(jax.random.fold_in(own, 1), rows)]
    turn = jax.random.randint(jax.random.fold_in(own, 2), (rows, 1), 0, top)
    return jnp.take_along_axis(grid, (jnp.arange(top)[None, :] + turn) % top, axis=1)


def shares(number_of, total, limit, skew, full):
    portions = [(1 << 20) // math.isqrt(rank ** skew) + 1 for rank in range(1, number_of + 1)]
    largest = limit if full else min(limit, max(-(-total // number_of), total * portions[0] // sum(portions)))
    least = 1 if total - largest >= number_of - 1 else 0
    given, spare = [largest] + [least] * (number_of - 1), total - largest - least * (number_of - 1)
    while spare > 0:
        candidates = [i for i in range(1, number_of) if given[i] < largest] or [i for i in range(1, number_of) if given[i] < limit]
        mass, budget = sum([portions[i] for i in candidates]), spare
        for i in candidates:
            addition = min(limit - given[i], max(1, budget * portions[i] // mass), spare)
            given[i] = given[i] + addition
            spare = spare - addition
    return np.array(given)


def normal_values(own_key, shape, scale, bound, shards=(), held_as=jnp.bfloat16):
    factor_of = steps_of(own_key, shape, shards, -0.22, 0.18) if shards else 1.0
    array = jax.random.normal(own_key, shape, jnp.float32) * scale * factor_of
    return jnp.minimum(jnp.maximum(array, -bound), bound).astype(held_as)


def noise_with(key, shape, deviation, reach, cuts, heavy, held_as=jnp.bfloat16):
    drawn = deviation * jax.random.normal(key, shape, jnp.float32)
    if cuts:
        drawn = drawn * steps_of(key, shape, cuts, -0.22, 0.18)
    return jnp.clip(strengthened(drawn, jax.random.fold_in(key, 3), *heavy), -reach, reach).astype(held_as)


def setup_inputs(seed: int = 0) -> dict:
    splits = jax.random.split(jax.random.key(seed), 6)
    grad_out = normal_values(splits[0], (TOKENS, D), 1.0, 6.0, ((0, 1024),))
    route_ids_keys = jax.random.split(jax.random.fold_in(splits[1], 1), TOKENS // TOK_DEV)
    route_ids_turns = jax.random.permutation(jax.random.fold_in(splits[1], 3), TOKENS // TOK_DEV)
    route_ids = jax.vmap(lambda own, number: shared_out(jax.random.fold_in(splits[1], 2), own, number, TOK_DEV, EXPERTS, TOP, CAP, 2))(route_ids_keys, route_ids_turns).reshape((TOKENS, TOP))
    route_probs = jnp.clip(jnp.exp(math.log(0.3) - 3.4011974 * jax.random.uniform(splits[2], (TOKENS, TOP), jnp.float32) ** steps_of(splits[2], (TOKENS, TOP), ((0, 1024),), -0.2, 0.2)), 0.01, 0.3)
    hidden = noise_with(splits[3], (N_DP, N_EXPERT, EXPERTS, CAP, H), 0.3, 2.0, ((0, 16), (2, 64)), (0, 4, 16, 2.0))
    w_down = normal_values(splits[4], (EXPERTS, H, D), H ** -0.5, 0.21875, ((0, 64),))
    return {"grad_out": grad_out, "route_ids": route_ids, "route_probs": route_probs, "hidden": hidden, "w_down": w_down}


def slots_of(route_blocks):
    hits = (route_blocks[..., None] == jnp.arange(EXPERTS, dtype=jnp.int32)).astype(jnp.int32).sum(2)
    before = jnp.cumsum(hits, axis=1) - hits
    return jnp.take_along_axis(before, route_blocks, axis=2)


def reference(grad_out, route_ids, route_probs, hidden, w_down):
    blocks = N_DP * N_EXPERT
    total = jnp.sum(route_probs, axis=1, keepdims=True)
    gates = route_probs / total
    gate_word = lax.optimization_barrier(gates.astype(jnp.bfloat16)).astype(jnp.float32)
    route_blocks = route_ids.reshape(blocks, TOK_DEV, TOP)
    slot = slots_of(route_blocks)
    block_index = jnp.arange(blocks, dtype=jnp.int32)[:, None, None]
    replica = block_index // N_EXPERT
    source = block_index % N_EXPERT
    per_expert = N_DP * N_EXPERT * CAP
    flat = (((route_blocks * N_DP + replica) * N_EXPERT + source) * CAP + slot).reshape(-1).astype(jnp.int32)
    pairs_all = TOKENS * TOP
    inverse = jnp.full((EXPERTS * per_expert,), pairs_all, jnp.int32).at[flat].set(jnp.arange(pairs_all, dtype=jnp.int32))
    gate_flat = gate_word.reshape(-1)

    def expert_step(index):
        picked = lax.dynamic_slice_in_dim(inverse, index * per_expert, per_expert)
        live = picked < pairs_all
        safe = jnp.where(live, picked, 0).astype(jnp.int32)
        rows = jnp.where(live[:, None], grad_out[safe // TOP], jnp.zeros((), jnp.bfloat16))
        factor = jnp.where(live, gate_flat[safe], jnp.zeros((), gate_flat.dtype))
        weight = lax.dynamic_index_in_dim(w_down, index, 0, keepdims=False)
        acts = lax.dynamic_index_in_dim(hidden, index, 2, keepdims=False).reshape(per_expert, H)
        raw = jnp.dot(rows, weight.T, preferred_element_type=jnp.float32)
        grad_hidden = (factor[:, None] * raw).astype(jnp.bfloat16)
        gate_grad = jnp.sum(raw * acts.astype(jnp.float32), axis=1)
        scaled = (factor[:, None] * rows.astype(jnp.float32)).astype(jnp.bfloat16)
        terms = jnp.einsum("prh,prd->phd", acts.reshape(N_DP, -1, H).astype(jnp.float32),
                           scaled.reshape(N_DP, -1, D).astype(jnp.float32))
        rounded = lax.optimization_barrier(terms.astype(jnp.bfloat16)).astype(jnp.float32)
        return grad_hidden, gate_grad, jnp.sum(rounded, axis=0)

    hidden_grads, gate_grads, weight_terms = lax.map(expert_step, jnp.arange(EXPERTS, dtype=jnp.int32))
    hidden_grad = hidden_grads.reshape(EXPERTS, N_DP, N_EXPERT, CAP, H).transpose(1, 2, 0, 3, 4)
    picked_grad = gate_grads.reshape(-1)[flat].reshape(TOKENS, TOP)
    prob_grad = (picked_grad - jnp.sum(gates * picked_grad, axis=1, keepdims=True)) / total
    weight_grad = weight_terms.transpose(1, 0, 2)
    return hidden_grad, prob_grad, weight_grad
```

```python
import functools

import jax
import jax.numpy as jnp
from jax import lax
from jax.experimental import pallas as pl
from jax.experimental.pallas import tpu as pltpu
from jax.sharding import PartitionSpec as P

MESH = pl.DeviceIdType.MESH
F32 = jnp.float32
BF16 = jnp.bfloat16
WIDTHS = (512, 512, 512, 512)
STARTS = tuple(sum(WIDTHS[:i]) for i in range(len(WIDTHS)))
CHUNKS = len(WIDTHS)
SIDE = 8
GROUPS = 64
SLOTS = 8
TOK = 128
H = 768
D = 2048
PART = 48


def kernel(
    grad_ref, ids_ref, probs_ref, hid_ref, w_ref,
    hg_ref, prob_ref, wg_ref,
    grad, wv, hid, hid_t, pick, rows, acc, hg, ret_out, ret_in, ret,
    send, recv, term, sib, out_buf, in_buf, wg,
    load_sem, a2a_send, a2a_recv, own_sem, sib_send, sib_recv, ring_send, ring_recv,
    ret_send, ret_recv, ret_own, store_sem,
):
    me = lax.axis_index("expert")
    dp = lax.axis_index("dp")
    mx, mz = me // SIDE, me % SIDE
    core = dp % 2
    y = dp // 2
    twin = dp + 1 - 2 * core
    ways = ((dp + 2) % 16, (dp + 14) % 16)

    def peer(k):
        dx, dz = k % SIDE, (k // SIDE + k) % SIDE
        return ((mx + dx) % SIDE) * SIDE + (mz + dz) % SIDE

    loads = [
        pltpu.make_async_copy(grad_ref, grad, load_sem.at[0]),
        pltpu.make_async_copy(hid_ref, hid, load_sem.at[1]),
        pltpu.make_async_copy(w_ref, wv, load_sem.at[2]),
    ]
    for load in loads:
        load.start()

    barrier = pltpu.get_barrier_semaphore()

    def greet(k, carry):
        pl.semaphore_signal(barrier, inc=1, device_id={"expert": peer(k)}, device_id_type=MESH)
        return carry

    lax.fori_loop(1, GROUPS, greet, 0)
    for other in (twin, *ways):
        pl.semaphore_signal(barrier, inc=1, device_id={"dp": other}, device_id_type=MESH)

    ids = [ids_ref[k : k + 1, :] for k in range(2)]
    probs = [probs_ref[k : k + 1, :] for k in range(2)]
    total = probs[0] + probs[1]
    gates = [p / total for p in probs]
    words = [g.astype(BF16).astype(F32) for g in gates]
    named = lax.broadcasted_iota(jnp.int32, (2 * GROUPS, TOK), 0)
    is_expert = [(named == i).astype(F32) for i in ids]
    earlier = (
        lax.broadcasted_iota(jnp.int32, (TOK, TOK), 0) < lax.broadcasted_iota(jnp.int32, (TOK, TOK), 1)
    ).astype(F32)
    before = jnp.dot(
        (is_expert[0] + is_expert[1]).astype(BF16), earlier.astype(BF16), preferred_element_type=F32
    )
    slot = [jnp.sum(before * i, axis=0, keepdims=True).astype(jnp.int32) for i in is_expert]
    place = [i * 4 + s for i, s in zip(ids, slot)]
    where = lax.broadcasted_iota(jnp.int32, (GROUPS * SLOTS, TOK), 0)
    pick[...] = (
        jnp.where(where == place[0], words[0], 0.0) + jnp.where(where == place[1], words[1], 0.0)
    ).astype(BF16)

    loads[0].wait()

    def fill(c):
        cols = slice(STARTS[c], STARTS[c] + WIDTHS[c])

        def group(i, carry):
            at = pl.multiple_of(i * 128, 128)
            got = jnp.dot(pick[pl.ds(at, 128), :], grad[:, cols], preferred_element_type=F32)
            send[c][pl.ds(i * 16, 16)] = got.reshape(16, SLOTS, WIDTHS[c]).astype(BF16)
            return carry

        lax.fori_loop(0, 4, group, 0)

    def launch(c):
        def one(k, carry):
            to = peer(k)
            pltpu.make_async_remote_copy(
                send[c].at[to], recv[c].at[me], a2a_send.at[c], a2a_recv.at[c],
                device_id={"expert": to}, device_id_type=MESH,
            ).start()
            return carry

        lax.fori_loop(1, GROUPS, one, 0)
        pltpu.make_async_copy(send[c].at[me], recv[c].at[me], own_sem.at[c]).start()

    def all_pairs(c):
        return pltpu.make_async_remote_copy(
            send[c].at[pl.ds(0, GROUPS - 1)], recv[c].at[pl.ds(0, GROUPS - 1)], a2a_send.at[c], a2a_recv.at[c],
            device_id={"expert": me}, device_id_type=MESH,
        )

    fill(0)
    pl.semaphore_wait(barrier, GROUPS - 1 + 3)
    launch(0)
    for c in range(1, CHUNKS):
        fill(c)
        launch(c)

    loads[1].wait()

    def turn(i, carry):
        at = pl.multiple_of(i * 128, 128)
        for e in range(2):
            hid_t[e, pl.ds(at, 128), :] = hid[e, :, pl.ds(at, 128)].astype(F32).T.astype(BF16)
        return carry

    lax.fori_loop(0, H // 128, turn, 0)
    loads[2].wait()

    def arrive(c):
        all_pairs(c).wait_recv()
        pltpu.make_async_copy(send[c].at[me], recv[c].at[me], own_sem.at[c]).wait()

    low = lax.broadcasted_iota(jnp.int32, (32, 8, 128), 1) < 4

    def part(c):
        def tile(n, carry):
            at = pl.multiple_of(n * 128, 128)
            got = recv[c][:, :, pl.ds(at, 128)].astype(F32).reshape(32, 2, 8, 128)
            even, odd = got[:, 0], got[:, 1]
            first = jnp.where(low, even, pltpu.roll(odd, 4, 1))
            second = jnp.where(low, pltpu.roll(even, 4, 1), odd)
            rows[0, :, pl.ds(at, 128)] = first.reshape(256, 128).astype(BF16)
            rows[1, :, pl.ds(at, 128)] = second.reshape(256, 128).astype(BF16)
            return carry

        lax.fori_loop(0, WIDTHS[c] // 128, tile, 0)

    def twin_copy(c, e):
        return pltpu.make_async_remote_copy(
            term[c].at[e, :, 1 - core], sib[c].at[e], sib_send.at[c, e], sib_recv.at[c, e],
            device_id={"dp": twin}, device_id_type=MESH,
        )

    def terms(c):
        for e in range(2):
            def tile(n, carry):
                at = pl.multiple_of(n * 256, 256)
                for m in range(2):
                    got = jnp.dot(
                        hid_t[e, m * 384 : (m + 1) * 384, :], rows[e, :, pl.ds(at, 256)], preferred_element_type=F32
                    )
                    term[c][e, m * 4 : (m + 1) * 4, :, :, pl.ds(at, 256)] = got.astype(BF16).reshape(4, 2, PART, 256)
                return carry

            lax.fori_loop(0, WIDTHS[c] // 256, tile, 0)
            twin_copy(c, e).start()

    def raws(c):
        cols = slice(STARTS[c], STARTS[c] + WIDTHS[c])
        for e in range(2):
            def tile(j, carry):
                at = pl.multiple_of(j * 256, 256)
                got = lax.dot_general(
                    rows[e, :, 0 : WIDTHS[c]], wv[e, pl.ds(at, 256), cols], (((1,), (1,)), ((), ())),
                    preferred_element_type=F32,
                )
                if c == 0:
                    acc[e, :, pl.ds(at, 256)] = got
                else:
                    acc[e, :, pl.ds(at, 256)] += got
                return carry

            lax.fori_loop(0, H // 256, tile, 0)

    def ring_copy(c, way, step):
        span = pl.ds(way, 1) if step == 0 else pl.ds(0, 2)
        return pltpu.make_async_remote_copy(
            out_buf[c].at[way, step, span], in_buf[c].at[way, step, span],
            ring_send.at[c, way, step], ring_recv.at[c, way, step],
            device_id={"dp": ways[way]}, device_id_type=MESH,
        )

    def chip_sum(c, e, at):
        return term[c][e, at, core].astype(F32) + sib[c][e, at].astype(F32)

    def ring(c, step):
        if step == 0:
            for e in range(2):
                twin_copy(c, e).wait_recv()
        for way in range(2):
            if step > 0:
                ring_copy(c, way, step - 1).wait_recv()
            target = (y + 4 - step) % SIDE if way == 0 else (y + 4 + step) % SIDE
            for e in range(2):
                if step == 0 and e != way:
                    continue
                value = chip_sum(c, e, target)
                if step > 1 or (step == 1 and e == way):
                    value = value + in_buf[c][way, step - 1, e].astype(F32)
                out_buf[c][way, step, e] = value.astype(BF16)
            ring_copy(c, way, step).start()

    def store_wg(c):
        cols = pl.ds(STARTS[c], WIDTHS[c])
        return pltpu.make_async_copy(wg.at[:, :, cols], wg_ref.at[:, :, cols], store_sem.at[c])

    def finish(c):
        for way in range(2):
            ring_copy(c, way, 3).wait_recv()
        for e in range(2):
            value = chip_sum(c, e, y) + in_buf[c][0, 3, e].astype(F32) + in_buf[c][1, 3, e].astype(F32)
            wg[e, :, STARTS[c] : STARTS[c] + WIDTHS[c]] = value
        store_wg(c).start()

    def ret_copies():
        return pltpu.make_async_remote_copy(
            ret_out.at[pl.ds(0, GROUPS - 1)], ret_in.at[pl.ds(0, GROUPS - 1)], ret_send, ret_recv,
            device_id={"expert": me}, device_id_type=MESH,
        )

    def store_hg():
        return pltpu.make_async_copy(hg, hg_ref, store_sem.at[CHUNKS])

    def answer():
        row = lax.broadcasted_iota(jnp.int32, (256, 128), 0)
        lane = lax.broadcasted_iota(jnp.int32, (256, 128), 1)
        source = lax.broadcasted_iota(jnp.int32, (GROUPS, 256), 0)
        of_source = (lax.broadcasted_iota(jnp.int32, (GROUPS, 256), 1) // 4 == source).astype(F32)
        both = jnp.zeros((GROUPS, 128), F32)
        for e in range(2):
            dots = jnp.sum(acc[e] * hid[e].astype(F32), axis=1, keepdims=True)
            spread = jnp.where(lane == 4 * e + row % 4, dots, 0.0)
            both = both + jnp.dot(
                of_source, spread, preferred_element_type=F32, precision=lax.Precision.HIGHEST
            )
            hg[e] = acc[e].astype(BF16)
        for g in range(GROUPS):
            ret_out[g] = both[g : g + 1, :]

        def one(k, carry):
            to = peer(k)
            pltpu.make_async_remote_copy(
                ret_out.at[to], ret_in.at[me], ret_send, ret_recv, device_id={"expert": to}, device_id_type=MESH
            ).start()
            return carry

        lax.fori_loop(1, GROUPS, one, 0)
        pltpu.make_async_copy(ret_out.at[me], ret_in.at[me], ret_own).start()
        store_hg().start()

    def gate_gradients():
        ret_copies().wait_recv()
        pltpu.make_async_copy(ret_out.at[me], ret_in.at[me], ret_own).wait()
        for g in range(GROUPS):
            ret[g : g + 1, :] = ret_in[g]
        got = ret[...]
        group = lax.broadcasted_iota(jnp.int32, (GROUPS, TOK), 0)
        lane = lax.broadcasted_iota(jnp.int32, (128, TOK), 0)
        picked = []
        for k in range(2):
            here = (group == place[k] // SLOTS).astype(F32)
            wide = lax.dot_general(
                got, here, (((0,), (0,)), ((), ())), preferred_element_type=F32, precision=lax.Precision.HIGHEST
            )
            scaled = jnp.sum(jnp.where(lane == place[k] % SLOTS, wide, 0.0), axis=0, keepdims=True)
            picked.append(scaled / words[k])
        mean = gates[0] * picked[0] + gates[1] * picked[1]
        for k in range(2):
            prob_ref[k : k + 1, :] = (picked[k] - mean) / total

    def work(c):
        arrive(c)
        part(c)
        terms(c)
        raws(c)

    last = CHUNKS - 1
    work(0)
    for c in range(1, CHUNKS):
        for step in range(3):
            ring(c - 1, step)
        work(c)
        ring(c - 1, 3)
        if c < last:
            finish(c - 1)
    ring(last, 0)
    answer()
    finish(last - 1)
    for step in range(1, 4):
        ring(last, step)
    gate_gradients()
    finish(last)

    for c in range(CHUNKS):
        all_pairs(c).wait_send()
        for e in range(2):
            twin_copy(c, e).wait_send()
        for way in range(2):
            for step in range(4):
                ring_copy(c, way, step).wait_send()
        store_wg(c).wait()
    ret_copies().wait_send()
    store_hg().wait()


def body(grad_out, route_ids, route_probs, hidden, w_down):
    hid = hidden[0].transpose(1, 0, 2, 3).reshape(2, 256, H)
    any_space = pl.BlockSpec(memory_space=pl.ANY)
    vmem = pl.BlockSpec(memory_space=pltpu.VMEM)
    dma = pltpu.SemaphoreType.DMA
    hg, prob, wg = pl.pallas_call(
        kernel,
        out_shape=(
            jax.ShapeDtypeStruct((2, 256, H), BF16),
            jax.ShapeDtypeStruct((2, TOK), F32),
            jax.ShapeDtypeStruct((2, PART, D), F32),
        ),
        in_specs=[any_space, vmem, vmem, any_space, any_space],
        out_specs=(any_space, vmem, any_space),
        scratch_shapes=[
            pltpu.VMEM((TOK, D), BF16),
            pltpu.VMEM((2, H, D), BF16),
            pltpu.VMEM((2, 256, H), BF16),
            pltpu.VMEM((2, H, 256), BF16),
            pltpu.VMEM((GROUPS * SLOTS, TOK), BF16),
            pltpu.VMEM((2, 256, max(WIDTHS)), BF16),
            pltpu.VMEM((2, 256, H), F32),
            pltpu.VMEM((2, 256, H), BF16),
            pltpu.VMEM((GROUPS, 1, 128), F32),
            pltpu.VMEM((GROUPS, 1, 128), F32),
            pltpu.VMEM((GROUPS, 128), F32),
            [pltpu.VMEM((GROUPS, SLOTS, w), BF16) for w in WIDTHS],
            [pltpu.VMEM((GROUPS, SLOTS, w), BF16) for w in WIDTHS],
            [pltpu.VMEM((2, SIDE, 2, PART, w), BF16) for w in WIDTHS],
            [pltpu.VMEM((2, SIDE, PART, w), BF16) for w in WIDTHS],
            [pltpu.VMEM((2, 4, 2, PART, w), BF16) for w in WIDTHS],
            [pltpu.VMEM((2, 4, 2, PART, w), BF16) for w in WIDTHS],
            pltpu.VMEM((2, PART, D), F32),
            dma((3,)),
            dma((CHUNKS,)),
            dma((CHUNKS,)),
            dma((CHUNKS,)),
            dma((CHUNKS, 2)),
            dma((CHUNKS, 2)),
            dma((CHUNKS, 2, 4)),
            dma((CHUNKS, 2, 4)),
            dma,
            dma,
            dma,
            dma((CHUNKS + 1,)),
        ],
        compiler_params=pltpu.CompilerParams(
            collective_id=0, has_side_effects=True, vmem_limit_bytes=56 * 2**20
        ),
        name="routed_backward",
    )(grad_out, route_ids.T, route_probs.T, hid, w_down)
    hidden_grad = hg.reshape(2, GROUPS, 4, H).transpose(1, 0, 2, 3)[None]
    return hidden_grad, prob.T, wg.transpose(1, 0, 2)


def solution(mesh):
    in_specs = (
        P(("dp", "expert"), None),
        P(("dp", "expert"), None),
        P(("dp", "expert"), None),
        P("dp", None, "expert", None, None),
        P("expert", None, None),
    )
    out_specs = (
        P("dp", None, "expert", None, None),
        P(("dp", "expert"), None),
        P("dp", "expert", None),
    )
    return jax.shard_map(body, mesh=mesh, in_specs=in_specs, out_specs=out_specs, check_vma=False)
```

```python
import jax
import jax.numpy as jnp
from jax import lax
from jax.experimental import pallas as pl
from jax.experimental.pallas import tpu as pltpu
from jax.sharding import PartitionSpec as P

MESH = pl.DeviceIdType.MESH
F32 = jnp.float32
BF16 = jnp.bfloat16
WIDTHS = (512, 512, 512, 512)
STARTS = tuple(sum(WIDTHS[:i]) for i in range(len(WIDTHS)))
CHUNKS = len(WIDTHS)
UNITS = ((0, 0, 512), (1, 0, 512), (2, 0, 512), (3, 0, 256), (3, 256, 256))
WINDOW = 8
BATCHES = tuple((c, k, k + 4096 // w) for c, w in enumerate(WIDTHS) for k in range(0, 64, 4096 // w))
ENDS = tuple(sum(w // 64 for w in WIDTHS[: c + 1]) for c in range(len(WIDTHS)))
SIDE = 8
GROUPS = 64
SLOTS = 8
TOK = 128
H = 768
D = 2048
PART = 48


def kernel(
    grad_ref, ids_ref, probs_ref, hid_ref, w_ref,
    hg_ref, prob_ref, wg_ref,
    grad, wv, hid_raw, hid, hid_t, pick, rows, acc, hg, ret_out, ret_in, ret,
    send, recv, term, sib, out_buf, in_buf, wg,
    load_sem, a2a_send, a2a_recv, own_sem, sib_send, sib_recv, hop_send, hop_recv,
    ret_send, ret_recv, ret_own, store_sem,
):
    me = lax.axis_index("expert")
    dp = lax.axis_index("dp")
    mx, mz = me // SIDE, me % SIDE
    core = dp % 2
    y = dp // 2
    twin = dp + 1 - 2 * core
    ways = (((dp + 2) % 16, (dp + 4) % 16), ((dp + 14) % 16, (dp + 12) % 16))

    def peer(k):
        dx, dz = k % SIDE, (k // SIDE + k) % SIDE
        return ((mx + dx) % SIDE) * SIDE + (mz + dz) % SIDE

    loads = [
        pltpu.make_async_copy(grad_ref, grad, load_sem.at[0]),
        pltpu.make_async_copy(hid_ref, hid_raw, load_sem.at[1]),
        pltpu.make_async_copy(w_ref, wv, load_sem.at[2]),
    ]
    for load in loads:
        load.start()

    barrier = pltpu.get_barrier_semaphore()

    def greet(k, carry):
        pl.semaphore_signal(barrier, inc=1, device_id={"expert": peer(k)}, device_id_type=MESH)
        return carry

    lax.fori_loop(1, GROUPS, greet, 0)
    for other in (twin, *ways[0], *ways[1]):
        pl.semaphore_signal(barrier, inc=1, device_id={"dp": other}, device_id_type=MESH)

    ids = [ids_ref[k : k + 1, :] for k in range(2)]
    probs = [probs_ref[k : k + 1, :] for k in range(2)]
    total = probs[0] + probs[1]
    gates = [p / total for p in probs]
    words = [g.astype(BF16).astype(F32) for g in gates]
    named = lax.broadcasted_iota(jnp.int32, (2 * GROUPS, TOK), 0)
    is_expert = [(named == i).astype(F32) for i in ids]
    earlier = (
        lax.broadcasted_iota(jnp.int32, (TOK, TOK), 0) < lax.broadcasted_iota(jnp.int32, (TOK, TOK), 1)
    ).astype(F32)
    before = jnp.dot(
        (is_expert[0] + is_expert[1]).astype(BF16), earlier.astype(BF16), preferred_element_type=F32
    )
    slot = [jnp.sum(before * i, axis=0, keepdims=True).astype(jnp.int32) for i in is_expert]
    place = [i * 4 + s for i, s in zip(ids, slot)]
    where = lax.broadcasted_iota(jnp.int32, (GROUPS * SLOTS, TOK), 0)
    pick[...] = (
        jnp.where(where == place[0], words[0], 0.0) + jnp.where(where == place[1], words[1], 0.0)
    ).astype(BF16)

    loads[0].wait()

    def fill(c):
        cols = slice(STARTS[c], STARTS[c] + WIDTHS[c])

        def group(i, carry):
            at = pl.multiple_of(i * 128, 128)
            got = jnp.dot(pick[pl.ds(at, 128), :], grad[:, cols], preferred_element_type=F32)
            send[c][pl.ds(i * 16, 16)] = got.reshape(16, SLOTS, WIDTHS[c]).astype(BF16)
            return carry

        lax.fori_loop(0, 4, group, 0)

    def pairs(c, b, count):
        return pltpu.make_async_remote_copy(
            send[c].at[pl.ds(0, count)], recv[c].at[pl.ds(0, count)], a2a_send.at[b], a2a_recv.at[c],
            device_id={"expert": me}, device_id_type=MESH,
        )

    def drain(b):
        c, start, stop = BATCHES[b]
        pairs(c, b, stop - max(start, 1)).wait_send()

    issued = [0]

    def pump(count=1):
        for _ in range(count):
            b = issued[0]
            if b == len(BATCHES):
                return
            issued[0] = b + 1
            if b >= WINDOW:
                drain(b - WINDOW)
            c, start, stop = BATCHES[b]

            def one(k, carry):
                to = peer(k)
                pltpu.make_async_remote_copy(
                    send[c].at[to], recv[c].at[me], a2a_send.at[b], a2a_recv.at[c],
                    device_id={"expert": to}, device_id_type=MESH,
                ).start()
                return carry

            lax.fori_loop(max(1, start), stop, one, 0)
            if start == 0:
                pltpu.make_async_copy(send[c].at[me], recv[c].at[me], own_sem.at[c]).start()

    fill(0)
    pl.semaphore_wait(barrier, GROUPS - 1 + 5)
    pump(WINDOW)
    for c in range(1, CHUNKS):
        fill(c)
        pump()

    loads[1].wait()

    def expand(i, carry):
        for e in range(2):
            four = [hid_raw[4 * i + j, e].astype(F32) for j in range(4)]
            hid[e, pl.ds(pl.multiple_of(16 * i, 16), 16), :] = jnp.concatenate(four, axis=0).astype(BF16)
        return carry

    lax.fori_loop(0, GROUPS // 4, expand, 0)

    def turn(i, carry):
        at = pl.multiple_of(i * 128, 128)
        for e in range(2):
            hid_t[e, pl.ds(at, 128), :] = hid[e, :, pl.ds(at, 128)].astype(F32).T.astype(BF16)
        return carry

    lax.fori_loop(0, H // 128, turn, 0)
    loads[2].wait()
    pump(ENDS[0] + WINDOW - issued[0])

    def arrive(c):
        pairs(c, 0, GROUPS - 1).wait_recv()
        pltpu.make_async_copy(send[c].at[me], recv[c].at[me], own_sem.at[c]).wait()

    low = lax.broadcasted_iota(jnp.int32, (32, 8, 128), 1) < 4

    def part(c):
        def tile(n, carry):
            at = pl.multiple_of(n * 128, 128)
            got = recv[c][:, :, pl.ds(at, 128)].astype(F32).reshape(32, 2, 8, 128)
            even, odd = got[:, 0], got[:, 1]
            first = jnp.where(low, even, pltpu.roll(odd, 4, 1))
            second = jnp.where(low, pltpu.roll(even, 4, 1), odd)
            rows[0, :, pl.ds(at, 128)] = first.reshape(256, 128).astype(BF16)
            rows[1, :, pl.ds(at, 128)] = second.reshape(256, 128).astype(BF16)
            return carry

        lax.fori_loop(0, WIDTHS[c] // 128, tile, 0)

    def twin_copy(c, e):
        return pltpu.make_async_remote_copy(
            term[c].at[e, :, 1 - core], sib[c].at[e], sib_send.at[c, e], sib_recv.at[c, e],
            device_id={"dp": twin}, device_id_type=MESH,
        )

    def terms(u):
        _, first, size = UNITS[u]
        for e in range(2):
            def tile(m, carry):
                got = jnp.dot(
                    hid_t[e, pl.ds(pl.multiple_of(m * 384, 384), 384), :], rows[e, :, first : first + size],
                    preferred_element_type=F32,
                )
                term[u][e, pl.ds(m * 4, 4)] = got.astype(BF16).reshape(4, 2, PART, size)
                return carry

            lax.fori_loop(0, 2, tile, 0)
            twin_copy(u, e).start()

    def raws(c):
        cols = slice(STARTS[c], STARTS[c] + WIDTHS[c])
        for e in range(2):
            def tile(j, carry):
                at = pl.multiple_of(j * 256, 256)
                got = lax.dot_general(
                    rows[e, :, 0 : WIDTHS[c]], wv[e, pl.ds(at, 256), cols], (((1,), (1,)), ((), ())),
                    preferred_element_type=F32,
                )
                if c == 0:
                    acc[e, :, pl.ds(at, 256)] = got
                else:
                    acc[e, :, pl.ds(at, 256)] += got
                return carry

            lax.fori_loop(0, H // 256, tile, 0)

    def hop(u, way, kind):
        span = pl.ds(way, 1) if kind == 0 else pl.ds(0, 2)
        return pltpu.make_async_remote_copy(
            out_buf[u].at[way, kind, span], in_buf[u].at[way, kind, span],
            hop_send.at[u, way, kind], hop_recv.at[u, way, kind],
            device_id={"dp": ways[way][1 if kind in (0, 3) else 0]}, device_id_type=MESH,
        )

    def target(way, distance):
        return (y + (distance if way == 0 else SIDE - distance)) % SIDE

    def chip_sum(c, e, at):
        return term[c][e, at, core].astype(F32) + sib[c][e, at].astype(F32)

    def spread(u):
        for e in range(2):
            twin_copy(u, e).wait_recv()
        for way in range(2):
            out_buf[u][way, 0, way] = chip_sum(u, way, target(way, 4)).astype(BF16)
            hop(u, way, 0).start()
            for kind, distance in ((1, 3), (2, 1)):
                for e in range(2):
                    out_buf[u][way, kind, e] = chip_sum(u, e, target(way, distance)).astype(BF16)
                hop(u, way, kind).start()

    def gather(u):
        for way in range(2):
            for kind in range(2):
                hop(u, way, kind).wait_recv()
            for e in range(2):
                value = chip_sum(u, e, target(way, 2)) + in_buf[u][way, 1, e].astype(F32)
                if e == way:
                    value = value + in_buf[u][way, 0, e].astype(F32)
                out_buf[u][way, 3, e] = value.astype(BF16)
            hop(u, way, 3).start()

    def store_wg(c):
        chunk, first, size = UNITS[c]
        cols = pl.ds(STARTS[chunk] + first, size)
        return pltpu.make_async_copy(wg.at[:, :, cols], wg_ref.at[:, :, cols], store_sem.at[c])

    def finish(c):
        chunk, first, size = UNITS[c]
        start = STARTS[chunk] + first
        for way in range(2):
            for kind in (2, 3):
                hop(c, way, kind).wait_recv()
        for e in range(2):
            value = chip_sum(c, e, y)
            for way in range(2):
                value = value + in_buf[c][way, 2, e].astype(F32) + in_buf[c][way, 3, e].astype(F32)
            wg[:, e, start : start + size] = value
        store_wg(c).start()

    def ret_copies():
        return pltpu.make_async_remote_copy(
            ret_out.at[pl.ds(0, GROUPS - 1)], ret_in.at[pl.ds(0, GROUPS - 1)], ret_send, ret_recv,
            device_id={"expert": me}, device_id_type=MESH,
        )

    def store_hg():
        return pltpu.make_async_copy(hg, hg_ref, store_sem.at[len(UNITS)])

    def answer():
        row = lax.broadcasted_iota(jnp.int32, (256, 128), 0)
        lane = lax.broadcasted_iota(jnp.int32, (256, 128), 1)
        source = lax.broadcasted_iota(jnp.int32, (GROUPS, 256), 0)
        of_source = (lax.broadcasted_iota(jnp.int32, (GROUPS, 256), 1) // 4 == source).astype(F32)
        both = jnp.zeros((GROUPS, 128), F32)
        for e in range(2):
            dots = jnp.sum(acc[e] * hid[e].astype(F32), axis=1, keepdims=True)
            spread = jnp.where(lane == 4 * e + row % 4, dots, 0.0)
            both = both + jnp.dot(
                of_source, spread, preferred_element_type=F32, precision=lax.Precision.HIGHEST
            )
        for g in range(GROUPS):
            ret_out[g] = both[g : g + 1, :]

        def one(k, carry):
            to = peer(k)
            pltpu.make_async_remote_copy(
                ret_out.at[to], ret_in.at[me], ret_send, ret_recv, device_id={"expert": to}, device_id_type=MESH
            ).start()
            return carry

        lax.fori_loop(1, GROUPS, one, 0)
        pltpu.make_async_copy(ret_out.at[me], ret_in.at[me], ret_own).start()

    def collect():
        def eight(i, carry):
            at = pl.multiple_of(8 * i, 8)
            for e in range(2):
                both = acc[e, pl.ds(at, 8), :]
                for j in range(2):
                    hg[2 * i + j, e] = both[4 * j : 4 * j + 4, :].astype(BF16)
            return carry

        lax.fori_loop(0, GROUPS // 2, eight, 0)
        store_hg().start()

    def gate_gradients():
        ret_copies().wait_recv()
        pltpu.make_async_copy(ret_out.at[me], ret_in.at[me], ret_own).wait()
        for g in range(GROUPS):
            ret[g : g + 1, :] = ret_in[g]
        got = ret[...]
        group = lax.broadcasted_iota(jnp.int32, (GROUPS, TOK), 0)
        lane = lax.broadcasted_iota(jnp.int32, (128, TOK), 0)
        picked = []
        for k in range(2):
            here = (group == place[k] // SLOTS).astype(F32)
            wide = lax.dot_general(
                got, here, (((0,), (0,)), ((), ())), preferred_element_type=F32, precision=lax.Precision.HIGHEST
            )
            scaled = jnp.sum(jnp.where(lane == place[k] % SLOTS, wide, 0.0), axis=0, keepdims=True)
            picked.append(scaled / words[k])
        mean = gates[0] * picked[0] + gates[1] * picked[1]
        for k in range(2):
            prob_ref[k : k + 1, :] = (picked[k] - mean) / total

    def begin(c):
        pump(ENDS[c] + WINDOW - issued[0])
        arrive(c)
        part(c)

    for c in range(3):
        begin(c)
        terms(c)
        pump()
        raws(c)
        pump()
        if c >= 1:
            gather(c - 1)
        pump(2)
        spread(c)
        pump(2)
        if c >= 1:
            finish(c - 1)
    begin(3)
    terms(3)
    gather(2)
    terms(4)
    spread(3)
    raws(3)
    spread(4)
    answer()
    finish(2)
    gather(3)
    collect()
    gather(4)
    finish(3)
    gate_gradients()
    finish(4)

    for b in range(len(BATCHES) - WINDOW, len(BATCHES)):
        drain(b)
    for c in range(len(UNITS)):
        for e in range(2):
            twin_copy(c, e).wait_send()
        for way in range(2):
            for kind in range(4):
                hop(c, way, kind).wait_send()
        store_wg(c).wait()
    ret_copies().wait_send()
    store_hg().wait()


def body(grad_out, route_ids, route_probs, hidden, w_down):
    any_space = pl.BlockSpec(memory_space=pl.ANY)
    vmem = pl.BlockSpec(memory_space=pltpu.VMEM)
    dma = pltpu.SemaphoreType.DMA
    hg, prob, wg = pl.pallas_call(
        kernel,
        out_shape=(
            jax.ShapeDtypeStruct((GROUPS, 2, 4, H), BF16),
            jax.ShapeDtypeStruct((2, TOK), F32),
            jax.ShapeDtypeStruct((PART, 2, D), F32),
        ),
        in_specs=[any_space, vmem, vmem, any_space, any_space],
        out_specs=(any_space, vmem, any_space),
        scratch_shapes=[
            pltpu.VMEM((TOK, D), BF16),
            pltpu.VMEM((2, H, D), BF16),
            pltpu.VMEM((GROUPS, 2, 4, H), BF16),
            pltpu.VMEM((2, 256, H), BF16),
            pltpu.VMEM((2, H, 256), BF16),
            pltpu.VMEM((GROUPS * SLOTS, TOK), BF16),
            pltpu.VMEM((2, 256, max(WIDTHS)), BF16),
            pltpu.VMEM((2, 256, H), F32),
            pltpu.VMEM((GROUPS, 2, 4, H), BF16),
            pltpu.VMEM((GROUPS, 1, 128), F32),
            pltpu.VMEM((GROUPS, 1, 128), F32),
            pltpu.VMEM((GROUPS, 128), F32),
            [pltpu.VMEM((GROUPS, SLOTS, w), BF16) for w in WIDTHS],
            [pltpu.VMEM((GROUPS, SLOTS, w), BF16) for w in WIDTHS],
            [pltpu.VMEM((2, SIDE, 2, PART, w), BF16) for _, _, w in UNITS],
            [pltpu.VMEM((2, SIDE, PART, w), BF16) for _, _, w in UNITS],
            [pltpu.VMEM((2, 4, 2, PART, w), BF16) for _, _, w in UNITS],
            [pltpu.VMEM((2, 4, 2, PART, w), BF16) for _, _, w in UNITS],
            pltpu.VMEM((PART, 2, D), F32),
            dma((3,)),
            dma((len(BATCHES),)),
            dma((CHUNKS,)),
            dma((CHUNKS,)),
            dma((len(UNITS), 2)),
            dma((len(UNITS), 2)),
            dma((len(UNITS), 2, 4)),
            dma((len(UNITS), 2, 4)),
            dma,
            dma,
            dma,
            dma((len(UNITS) + 1,)),
        ],
        compiler_params=pltpu.CompilerParams(
            collective_id=0, has_side_effects=True, vmem_limit_bytes=56 * 2**20
        ),
        name="routed_backward",
    )(grad_out, route_ids.T, route_probs.T, hidden[0], w_down)
    return hg[None], prob.T, wg


def solution(mesh):
    in_specs = (
        P(("dp", "expert"), None),
        P(("dp", "expert"), None),
        P(("dp", "expert"), None),
        P("dp", None, "expert", None, None),
        P("expert", None, None),
    )
    out_specs = (
        P("dp", None, "expert", None, None),
        P(("dp", "expert"), None),
        P("dp", "expert", None),
    )
    return jax.shard_map(body, mesh=mesh, in_specs=in_specs, out_specs=out_specs, check_vma=False)
```

```python
import jax
import jax.numpy as jnp
from jax import lax
from jax.experimental import pallas as pl
from jax.experimental.pallas import tpu as pltpu
from jax.sharding import PartitionSpec as P

MESH = pl.DeviceIdType.MESH
F32 = jnp.float32
BF16 = jnp.bfloat16
WIDTHS = (512, 512, 512, 384, 128)
STARTS = tuple(sum(WIDTHS[:i]) for i in range(len(WIDTHS)))
CHUNKS = len(WIDTHS)
UNITS = ((0, 0, 512), (1, 0, 512), (2, 0, 512), (3, 0, 384), (4, 0, 128))
WINDOW = 8
PAIRS = tuple(32 if w == 128 else 8 for w in WIDTHS)
BATCHES = tuple((c, k, k + n) for c, n in enumerate(PAIRS) for k in range(0, 64, n))
ENDS = tuple(sum(64 // n for n in PAIRS[: c + 1]) for c in range(len(WIDTHS)))
SIDE = 8
GROUPS = 64
SLOTS = 8
TOK = 128
H = 768
D = 2048
PART = 48


def kernel(
    grad_ref, ids_ref, probs_ref, hid_ref, w_ref,
    hg_ref, prob_ref, wg_ref,
    grad, wv, hid_raw, hid, hid_t, pick, rows, acc, hg, ret_out, ret_in, ret,
    send, recv, term, sib, out_buf, in_buf, wg,
    load_sem, a2a_send, a2a_recv, own_sem, sib_send, sib_recv, hop_send, hop_recv,
    ret_send, ret_recv, ret_own, store_sem,
):
    me = lax.axis_index("expert")
    dp = lax.axis_index("dp")
    mx, mz = me // SIDE, me % SIDE
    core = dp % 2
    y = dp // 2
    twin = dp + 1 - 2 * core
    ways = (((dp + 2) % 16, (dp + 4) % 16), ((dp + 14) % 16, (dp + 12) % 16))

    def peer(k):
        dx, dz = k % SIDE, (k // SIDE + k) % SIDE
        return ((mx + dx) % SIDE) * SIDE + (mz + dz) % SIDE

    loads = [
        pltpu.make_async_copy(grad_ref, grad, load_sem.at[0]),
        pltpu.make_async_copy(hid_ref, hid_raw, load_sem.at[1]),
        pltpu.make_async_copy(w_ref, wv, load_sem.at[2]),
    ]
    for load in loads:
        load.start()

    barrier = pltpu.get_barrier_semaphore()

    def greet(k, carry):
        pl.semaphore_signal(barrier, inc=1, device_id={"expert": peer(k)}, device_id_type=MESH)
        return carry

    lax.fori_loop(1, GROUPS, greet, 0)
    for other in (twin, *ways[0], *ways[1]):
        pl.semaphore_signal(barrier, inc=1, device_id={"dp": other}, device_id_type=MESH)

    ids = [ids_ref[k : k + 1, :] for k in range(2)]
    probs = [probs_ref[k : k + 1, :] for k in range(2)]
    total = probs[0] + probs[1]
    gates = [p / total for p in probs]
    words = [g.astype(BF16).astype(F32) for g in gates]
    named = lax.broadcasted_iota(jnp.int32, (2 * GROUPS, TOK), 0)
    is_expert = [(named == i).astype(F32) for i in ids]
    earlier = (
        lax.broadcasted_iota(jnp.int32, (TOK, TOK), 0) < lax.broadcasted_iota(jnp.int32, (TOK, TOK), 1)
    ).astype(F32)
    before = jnp.dot(
        (is_expert[0] + is_expert[1]).astype(BF16), earlier.astype(BF16), preferred_element_type=F32
    )
    slot = [jnp.sum(before * i, axis=0, keepdims=True).astype(jnp.int32) for i in is_expert]
    place = [i * 4 + s for i, s in zip(ids, slot)]
    where = lax.broadcasted_iota(jnp.int32, (GROUPS * SLOTS, TOK), 0)
    pick[...] = (
        jnp.where(where == place[0], words[0], 0.0) + jnp.where(where == place[1], words[1], 0.0)
    ).astype(BF16)

    loads[0].wait()

    def fill(c):
        cols = slice(STARTS[c], STARTS[c] + WIDTHS[c])

        def group(i, carry):
            at = pl.multiple_of(i * 128, 128)
            got = jnp.dot(pick[pl.ds(at, 128), :], grad[:, cols], preferred_element_type=F32)
            send[c][pl.ds(i * 16, 16)] = got.reshape(16, SLOTS, WIDTHS[c]).astype(BF16)
            return carry

        lax.fori_loop(0, 4, group, 0)

    def pairs(c, b, count):
        return pltpu.make_async_remote_copy(
            send[c].at[pl.ds(0, count)], recv[c].at[pl.ds(0, count)], a2a_send.at[b], a2a_recv.at[c],
            device_id={"expert": me}, device_id_type=MESH,
        )

    def drain(b):
        c, start, stop = BATCHES[b]
        pairs(c, b, stop - max(start, 1)).wait_send()

    issued = [0]

    def pump(count=1):
        for _ in range(count):
            b = issued[0]
            if b == len(BATCHES):
                return
            issued[0] = b + 1
            if b >= WINDOW:
                drain(b - WINDOW)
            c, start, stop = BATCHES[b]

            def one(k, carry):
                to = peer(k)
                pltpu.make_async_remote_copy(
                    send[c].at[to], recv[c].at[me], a2a_send.at[b], a2a_recv.at[c],
                    device_id={"expert": to}, device_id_type=MESH,
                ).start()
                return carry

            lax.fori_loop(max(1, start), stop, one, 0)
            if start == 0:
                pltpu.make_async_copy(send[c].at[me], recv[c].at[me], own_sem.at[c]).start()

    fill(0)
    pl.semaphore_wait(barrier, GROUPS - 1 + 5)
    pump(WINDOW)
    for c in range(1, CHUNKS):
        fill(c)
        pump()

    loads[1].wait()

    def expand(i, carry):
        for e in range(2):
            four = [hid_raw[4 * i + j, e].astype(F32) for j in range(4)]
            hid[e, pl.ds(pl.multiple_of(16 * i, 16), 16), :] = jnp.concatenate(four, axis=0).astype(BF16)
        return carry

    lax.fori_loop(0, GROUPS // 4, expand, 0)

    def turn(i, carry):
        at = pl.multiple_of(i * 128, 128)
        for e in range(2):
            hid_t[e, pl.ds(at, 128), :] = hid[e, :, pl.ds(at, 128)].astype(F32).T.astype(BF16)
        return carry

    lax.fori_loop(0, H // 128, turn, 0)
    loads[2].wait()
    pump(ENDS[0] + WINDOW - issued[0])

    def arrive(c):
        pairs(c, 0, GROUPS - 1).wait_recv()
        pltpu.make_async_copy(send[c].at[me], recv[c].at[me], own_sem.at[c]).wait()

    low = lax.broadcasted_iota(jnp.int32, (32, 8, 128), 1) < 4

    def part(c):
        def tile(n, carry):
            at = pl.multiple_of(n * 128, 128)
            got = recv[c][:, :, pl.ds(at, 128)].astype(F32).reshape(32, 2, 8, 128)
            even, odd = got[:, 0], got[:, 1]
            first = jnp.where(low, even, pltpu.roll(odd, 4, 1))
            second = jnp.where(low, pltpu.roll(even, 4, 1), odd)
            rows[0, :, pl.ds(at, 128)] = first.reshape(256, 128).astype(BF16)
            rows[1, :, pl.ds(at, 128)] = second.reshape(256, 128).astype(BF16)
            return carry

        lax.fori_loop(0, WIDTHS[c] // 128, tile, 0)

    def twin_copy(c, e):
        return pltpu.make_async_remote_copy(
            term[c].at[e, :, 1 - core], sib[c].at[e], sib_send.at[c, e], sib_recv.at[c, e],
            device_id={"dp": twin}, device_id_type=MESH,
        )

    def terms(u):
        _, first, size = UNITS[u]
        for e in range(2):
            def tile(m, carry):
                got = jnp.dot(
                    hid_t[e, pl.ds(pl.multiple_of(m * 384, 384), 384), :], rows[e, :, first : first + size],
                    preferred_element_type=F32,
                )
                term[u][e, pl.ds(m * 4, 4)] = got.astype(BF16).reshape(4, 2, PART, size)
                return carry

            lax.fori_loop(0, 2, tile, 0)
            twin_copy(u, e).start()

    def raws(c):
        cols = slice(STARTS[c], STARTS[c] + WIDTHS[c])
        for e in range(2):
            def tile(j, carry):
                at = pl.multiple_of(j * 256, 256)
                got = lax.dot_general(
                    rows[e, :, 0 : WIDTHS[c]], wv[e, pl.ds(at, 256), cols], (((1,), (1,)), ((), ())),
                    preferred_element_type=F32,
                )
                if c == 0:
                    acc[e, :, pl.ds(at, 256)] = got
                else:
                    acc[e, :, pl.ds(at, 256)] += got
                return carry

            lax.fori_loop(0, H // 256, tile, 0)

    def hop(u, way, kind):
        span = pl.ds(way, 1) if kind == 0 else pl.ds(0, 2)
        return pltpu.make_async_remote_copy(
            out_buf[u].at[way, kind, span], in_buf[u].at[way, kind, span],
            hop_send.at[u, way, kind], hop_recv.at[u, way, kind],
            device_id={"dp": ways[way][1 if kind in (0, 3) else 0]}, device_id_type=MESH,
        )

    def target(way, distance):
        return (y + (distance if way == 0 else SIDE - distance)) % SIDE

    def chip_sum(c, e, at):
        return term[c][e, at, core].astype(F32) + sib[c][e, at].astype(F32)

    def spread(u):
        for e in range(2):
            twin_copy(u, e).wait_recv()
        for way in range(2):
            out_buf[u][way, 0, way] = chip_sum(u, way, target(way, 4)).astype(BF16)
            hop(u, way, 0).start()
            for kind, distance in ((1, 3), (2, 1)):
                for e in range(2):
                    out_buf[u][way, kind, e] = chip_sum(u, e, target(way, distance)).astype(BF16)
                hop(u, way, kind).start()

    def gather(u):
        for way in range(2):
            for kind in range(2):
                hop(u, way, kind).wait_recv()
            for e in range(2):
                value = chip_sum(u, e, target(way, 2)) + in_buf[u][way, 1, e].astype(F32)
                if e == way:
                    value = value + in_buf[u][way, 0, e].astype(F32)
                out_buf[u][way, 3, e] = value.astype(BF16)
            hop(u, way, 3).start()

    def store_wg(c):
        chunk, first, size = UNITS[c]
        cols = pl.ds(STARTS[chunk] + first, size)
        return pltpu.make_async_copy(wg.at[:, :, cols], wg_ref.at[:, :, cols], store_sem.at[c])

    def finish(c):
        chunk, first, size = UNITS[c]
        start = STARTS[chunk] + first
        for way in range(2):
            for kind in (2, 3):
                hop(c, way, kind).wait_recv()
        for e in range(2):
            value = chip_sum(c, e, y)
            for way in range(2):
                value = value + in_buf[c][way, 2, e].astype(F32) + in_buf[c][way, 3, e].astype(F32)
            wg[:, e, start : start + size] = value
        store_wg(c).start()

    def ret_copies():
        return pltpu.make_async_remote_copy(
            ret_out.at[pl.ds(0, GROUPS - 1)], ret_in.at[pl.ds(0, GROUPS - 1)], ret_send, ret_recv,
            device_id={"expert": me}, device_id_type=MESH,
        )

    def store_hg():
        return pltpu.make_async_copy(hg, hg_ref, store_sem.at[len(UNITS)])

    def answer():
        row = lax.broadcasted_iota(jnp.int32, (256, 128), 0)
        lane = lax.broadcasted_iota(jnp.int32, (256, 128), 1)
        source = lax.broadcasted_iota(jnp.int32, (GROUPS, 256), 0)
        of_source = (lax.broadcasted_iota(jnp.int32, (GROUPS, 256), 1) // 4 == source).astype(F32)
        both = jnp.zeros((GROUPS, 128), F32)
        for e in range(2):
            dots = jnp.sum(acc[e] * hid[e].astype(F32), axis=1, keepdims=True)
            spread = jnp.where(lane == 4 * e + row % 4, dots, 0.0)
            both = both + jnp.dot(
                of_source, spread, preferred_element_type=F32, precision=lax.Precision.HIGHEST
            )
        for g in range(GROUPS):
            ret_out[g] = both[g : g + 1, :]

        def one(k, carry):
            to = peer(k)
            pltpu.make_async_remote_copy(
                ret_out.at[to], ret_in.at[me], ret_send, ret_recv, device_id={"expert": to}, device_id_type=MESH
            ).start()
            return carry

        lax.fori_loop(1, GROUPS, one, 0)
        pltpu.make_async_copy(ret_out.at[me], ret_in.at[me], ret_own).start()

    def collect():
        def eight(i, carry):
            at = pl.multiple_of(8 * i, 8)
            for e in range(2):
                both = acc[e, pl.ds(at, 8), :]
                for j in range(2):
                    hg[2 * i + j, e] = both[4 * j : 4 * j + 4, :].astype(BF16)
            return carry

        lax.fori_loop(0, GROUPS // 2, eight, 0)
        store_hg().start()

    def gate_gradients():
        ret_copies().wait_recv()
        pltpu.make_async_copy(ret_out.at[me], ret_in.at[me], ret_own).wait()
        for g in range(GROUPS):
            ret[g : g + 1, :] = ret_in[g]
        got = ret[...]
        group = lax.broadcasted_iota(jnp.int32, (GROUPS, TOK), 0)
        lane = lax.broadcasted_iota(jnp.int32, (128, TOK), 0)
        picked = []
        for k in range(2):
            here = (group == place[k] // SLOTS).astype(F32)
            wide = lax.dot_general(
                got, here, (((0,), (0,)), ((), ())), preferred_element_type=F32, precision=lax.Precision.HIGHEST
            )
            scaled = jnp.sum(jnp.where(lane == place[k] % SLOTS, wide, 0.0), axis=0, keepdims=True)
            picked.append(scaled / words[k])
        mean = gates[0] * picked[0] + gates[1] * picked[1]
        for k in range(2):
            prob_ref[k : k + 1, :] = (picked[k] - mean) / total

    def begin(c):
        pump(ENDS[c] + WINDOW - issued[0])
        arrive(c)
        part(c)

    for c in range(3):
        begin(c)
        terms(c)
        pump()
        raws(c)
        pump()
        if c >= 1:
            gather(c - 1)
        pump(2)
        spread(c)
        pump(2)
        if c >= 1:
            finish(c - 1)
    begin(3)
    terms(3)
    raws(3)
    gather(2)
    spread(3)
    begin(4)
    terms(4)
    raws(4)
    spread(4)
    answer()
    gather(3)
    finish(2)
    collect()
    gather(4)
    finish(3)
    gate_gradients()
    finish(4)

    for b in range(len(BATCHES) - WINDOW, len(BATCHES)):
        drain(b)
    for c in range(len(UNITS)):
        for e in range(2):
            twin_copy(c, e).wait_send()
        for way in range(2):
            for kind in range(4):
                hop(c, way, kind).wait_send()
        store_wg(c).wait()
    ret_copies().wait_send()
    store_hg().wait()


def body(grad_out, route_ids, route_probs, hidden, w_down):
    any_space = pl.BlockSpec(memory_space=pl.ANY)
    vmem = pl.BlockSpec(memory_space=pltpu.VMEM)
    dma = pltpu.SemaphoreType.DMA
    hg, prob, wg = pl.pallas_call(
        kernel,
        out_shape=(
            jax.ShapeDtypeStruct((GROUPS, 2, 4, H), BF16),
            jax.ShapeDtypeStruct((2, TOK), F32),
            jax.ShapeDtypeStruct((PART, 2, D), F32),
        ),
        in_specs=[any_space, vmem, vmem, any_space, any_space],
        out_specs=(any_space, vmem, any_space),
        scratch_shapes=[
            pltpu.VMEM((TOK, D), BF16),
            pltpu.VMEM((2, H, D), BF16),
            pltpu.VMEM((GROUPS, 2, 4, H), BF16),
            pltpu.VMEM((2, 256, H), BF16),
            pltpu.VMEM((2, H, 256), BF16),
            pltpu.VMEM((GROUPS * SLOTS, TOK), BF16),
            pltpu.VMEM((2, 256, max(WIDTHS)), BF16),
            pltpu.VMEM((2, 256, H), F32),
            pltpu.VMEM((GROUPS, 2, 4, H), BF16),
            pltpu.VMEM((GROUPS, 1, 128), F32),
            pltpu.VMEM((GROUPS, 1, 128), F32),
            pltpu.VMEM((GROUPS, 128), F32),
            [pltpu.VMEM((GROUPS, SLOTS, w), BF16) for w in WIDTHS],
            [pltpu.VMEM((GROUPS, SLOTS, w), BF16) for w in WIDTHS],
            [pltpu.VMEM((2, SIDE, 2, PART, w), BF16) for _, _, w in UNITS],
            [pltpu.VMEM((2, SIDE, PART, w), BF16) for _, _, w in UNITS],
            [pltpu.VMEM((2, 4, 2, PART, w), BF16) for _, _, w in UNITS],
            [pltpu.VMEM((2, 4, 2, PART, w), BF16) for _, _, w in UNITS],
            pltpu.VMEM((PART, 2, D), F32),
            dma((3,)),
            dma((len(BATCHES),)),
            dma((CHUNKS,)),
            dma((CHUNKS,)),
            dma((len(UNITS), 2)),
            dma((len(UNITS), 2)),
            dma((len(UNITS), 2, 4)),
            dma((len(UNITS), 2, 4)),
            dma,
            dma,
            dma,
            dma((len(UNITS) + 1,)),
        ],
        compiler_params=pltpu.CompilerParams(
            collective_id=0, has_side_effects=True, vmem_limit_bytes=56 * 2**20
        ),
        name="routed_backward",
    )(grad_out, route_ids.T, route_probs.T, hidden[0], w_down)
    return hg[None], prob.T, wg


def solution(mesh):
    in_specs = (
        P(("dp", "expert"), None),
        P(("dp", "expert"), None),
        P(("dp", "expert"), None),
        P("dp", None, "expert", None, None),
        P("expert", None, None),
    )
    out_specs = (
        P("dp", None, "expert", None, None),
        P(("dp", "expert"), None),
        P("dp", "expert", None),
    )
    return jax.shard_map(body, mesh=mesh, in_specs=in_specs, out_specs=out_specs, check_vma=False)
```
